256 devices in a mesh: gx: 16 (over z_hi, x), gy: 16 (over y, z_lo, core).
Axes of the slice: x: 4, y: 4, z: 8 (z_hi: 4, z_lo: 2; z = z_hi * 2 + z_lo), core: 2. Of those that a mesh axis runs over, the one named last changes fastest.
Arguments:
- site_frac: float32 [3, 32, 32, 128], P(None, 'gx', 'gy'), may hold values from 0 to 1
- dual_weight: float32 [32, 32, 128], P('gx', 'gy'), may hold values from -2.5 to 64
- target_mass: float32 [32, 32, 128], P('gx', 'gy'), may hold values from 0.2 to 0.8
- block_list: int32 [16, 16, 12], P('gx', 'gy'), may hold values from 0 to 35, as said below
- block_count: int32 [16, 16], P('gx', 'gy'), may hold values from 1 to 12, as said below
Outputs:
- new_dual: float32 [32, 32, 128], P('gx', 'gy')
- site_shift: float32 [3, 32, 32, 128], P(None, 'gx', 'gy')
- displacement: float32 [3, 64, 64, 256], P(None, 'gx', 'gy')
The draws below stay inside these ranges and needn't reach their ends.
Inputs may be any that keep to these rules, and one draw needn't show every extreme that they name: `block_list`: within one tile the 12 entries are distinct. The first block_count entries name halo slots whose blocks hold sites of that tile's neighbourhood. `block_count`: some tile uses all 12 entries.
All inputs are finite; a program needn't handle non-finite values.
Results may differ from the reference program's by a relative error of at most 0.0003.
Values sent between devices are 32-bit elements; how exact they have to be, the bound alone decides.
No kernel may reach another device: no remote copies, remote signals or barrier semaphores. Data moves between devices by JAX's collectives and lax.ppermute only.
A program may use at most 64 MiB of HBM per device.

```python
import jax
import jax.numpy as jnp
from jax import lax

TX = 4
TY = 4
Z = 256
SB_SIDE = 2
BLOCK = 128
K_MAX = 12
NBX = 32
NBY = 32
NX = 64
NY = 64
N_GX = 16
N_GY = 16


def layout_draw(key):
    base_key = jax.random.fold_in(key, 11)
    key_first = jax.random.fold_in(base_key, 0)
    key_pick = jax.random.fold_in(base_key, 2)
    key_order = jax.random.fold_in(base_key, 3)
    blocks = SB_SIDE * SB_SIDE
    lowest = blocks // 2
    living = jax.random.randint(key_first, (N_GX, N_GY), lowest, blocks + 1)
    chosen_tile = jax.random.randint(key_pick, (), 0, N_GX * N_GY)
    tile_serial = jnp.arange(N_GX * N_GY).reshape(N_GX, N_GY)
    living = jnp.where(tile_serial == chosen_tile, blocks, living)
    span_slots = 3 * SB_SIDE
    slot_ids = jnp.arange(span_slots * span_slots)
    slot_row = slot_ids // span_slots
    slot_col = slot_ids % span_slots
    near_x = (jnp.arange(N_GX)[:, None, None] + slot_row[None, None, :] // SB_SIDE - 1) % N_GX
    near_y = (jnp.arange(N_GY)[None, :, None] + slot_col[None, None, :] // SB_SIDE - 1) % N_GY
    inner_id = slot_row % SB_SIDE * SB_SIDE + slot_col % SB_SIDE
    usable = (inner_id[None, None, :] < living[near_x, near_y]).astype(jnp.int32)
    ranking = jax.random.randint(key_order, (N_GX, N_GY, span_slots * span_slots), 0, 1024)
    keyed_rank = usable * (1024 * span_slots * span_slots) + ranking * (span_slots * span_slots) + slot_ids[None, None, :]
    ignored, chosen_order = lax.top_k(keyed_rank, K_MAX)
    available = jnp.sum(usable, axis=-1)
    counts = jnp.minimum(jnp.minimum(available, K_MAX), (K_MAX * living + blocks - 1) // blocks)
    return (chosen_order.astype(jnp.int32), counts.astype(jnp.int32))


def draw_block_list(key, part):
    return layout_draw(key)[0]


def draw_block_count(key, part):
    return layout_draw(key)[1]


def draw_dual_weight(key, part):
    key_base = jax.random.fold_in(jax.random.fold_in(key, 23), 0)
    dims_shape = (NBX, NBY, BLOCK)
    return jnp.clip(0.5 * jax.random.normal(key_base, dims_shape, jnp.float32), -2.5, 2.5)


def block_levels(own_key, extent, cuts, least, largest):
    level, own = 1.0, jax.random.fold_in(own_key, 6)
    for dim, blocks in cuts:
        draws = jnp.exp(jax.random.uniform(jax.random.fold_in(own, dim), (blocks,), jnp.float32, least / len(cuts), largest / len(cuts)))
        level = level * jnp.repeat(draws, extent[dim] // blocks).reshape([-1 if axis == dim else 1 for axis in range(len(extent))])
    return level


def setup_inputs(seed: int = 0) -> dict:
    keys = jax.random.split(jax.random.key(seed), 6)
    site_frac = jnp.clip(1.0 * jax.random.uniform(keys[0], (3, NBX, NBY, BLOCK), jnp.float32) ** block_levels(keys[0], (3, NBX, NBY, BLOCK), ((1, 16), (2, 16)), -0.2, 0.2), 0.0, 1.0)
    dual_weight = draw_dual_weight(jax.random.fold_in(keys[5], 71), 0)
    target_mass = jnp.clip(0.2 + 0.6 * jax.random.uniform(keys[2], (NBX, NBY, BLOCK), jnp.float32) ** block_levels(keys[2], (NBX, NBY, BLOCK), ((0, 16), (1, 16)), -0.2, 0.2), 0.2, 0.8)
    block_list = draw_block_list(jax.random.fold_in(keys[5], 71), 0)
    block_count = draw_block_count(jax.random.fold_in(keys[5], 71), 0)
    return {"site_frac": site_frac, "dual_weight": dual_weight, "target_mass": target_mass, "block_list": block_list, "block_count": block_count}


entropy_scale = 0.5
step_rate = 0.5


def grid_points(first_row, how_many):
    serial = first_row + jnp.arange(how_many)
    cell_x = serial // (TY * Z)
    cell_y = (serial // Z) % TY
    cell_z = serial % Z
    return jnp.stack([cell_x, cell_y, cell_z]).astype(jnp.float32) + 0.5


def assign(points, chosen, usable, moments):
    spread = points[:, :, None] - chosen[:3, None, :]
    distance = spread[0] * spread[0] + spread[1] * spread[1] + spread[2] * spread[2]
    scores = jnp.where(usable[None, :], (chosen[3][None, :] - distance) / entropy_scale, -jnp.inf)
    peak_score = jnp.max(scores, axis=1, keepdims=True)
    weights = jnp.exp(scores - peak_score)
    shares = weights / jnp.sum(weights, axis=1, keepdims=True)
    masses = jnp.sum(shares, axis=0)
    if not moments:
        return masses, None, None
    moment = jnp.sum(shares[None] * spread, axis=1)
    offsets = -jnp.sum(shares[None] * spread, axis=2)
    return masses, moment, offsets


def wrapped(tile_pos, total_blocks):
    return (tile_pos * SB_SIDE - SB_SIDE + jnp.arange(3 * SB_SIDE)) % total_blocks


def tile_step(site_frac, duals, block_list, block_count, tile_id):
    tile_x = tile_id // N_GY
    tile_y = tile_id % N_GY
    row_ids = wrapped(tile_x, NBX)
    col_ids = wrapped(tile_y, NBY)
    fraction = site_frac[:, row_ids][:, :, col_ids]
    local_duals = duals[row_ids][:, col_ids]
    offset = (jnp.arange(3 * SB_SIDE) // SB_SIDE - 1).astype(jnp.float32)
    site_table = jnp.stack([fraction[0] * TX + offset[:, None, None] * TX,
                            fraction[1] * TY + offset[None, :, None] * TY,
                            fraction[2] * Z, local_duals])
    flat_table = site_table.reshape(4, 9 * SB_SIDE * SB_SIDE, BLOCK)
    chosen_ids = block_list[tile_x, tile_y]
    live_count = block_count[tile_x, tile_y]
    chosen = flat_table[:, chosen_ids].reshape(4, K_MAX * BLOCK)
    usable = jnp.arange(K_MAX * BLOCK) // BLOCK < live_count
    masses, moment, offsets = assign(grid_points(0, TX * TY * Z), chosen, usable, True)
    partials = jnp.concatenate([masses[None], moment], 0).reshape(4, K_MAX, BLOCK)
    partials = jnp.where((jnp.arange(K_MAX) < live_count)[None, :, None], partials, 0.0)
    summed = jnp.zeros((4, 9 * SB_SIDE * SB_SIDE, BLOCK), jnp.float32).at[:, chosen_ids].add(partials)
    return summed, offsets


def one_step(site_frac, duals, block_list, block_count):
    tile_total = N_GX * N_GY
    summed, offsets = lax.map(lambda tile_id: tile_step(site_frac, duals, block_list, block_count, tile_id),
                              jnp.arange(tile_total))
    tile_serial = jnp.arange(tile_total)
    row_ids = ((tile_serial // N_GY)[:, None] * SB_SIDE - SB_SIDE + jnp.arange(3 * SB_SIDE)[None, :]) % NBX
    col_ids = ((tile_serial % N_GY)[:, None] * SB_SIDE - SB_SIDE + jnp.arange(3 * SB_SIDE)[None, :]) % NBY
    pieces = summed.reshape(tile_total, 4, 3 * SB_SIDE, 3 * SB_SIDE, BLOCK).transpose(0, 2, 3, 1, 4)
    totals = jnp.zeros((NBX, NBY, 4, BLOCK), jnp.float32).at[row_ids[:, :, None], col_ids[:, None, :]].add(pieces)
    return totals.transpose(2, 0, 1, 3), offsets


def reference(site_frac, dual_weight, target_mass, block_list, block_count):
    totals, offsets = one_step(site_frac, dual_weight, block_list, block_count)
    dual_mid = dual_weight + step_rate * (target_mass - totals[0])
    totals, offsets = one_step(site_frac, dual_mid, block_list, block_count)
    new_dual = dual_mid + step_rate * (target_mass - totals[0])
    site_shift = totals[1:] / (totals[0] + target_mass)[None]
    displacement = offsets.reshape(N_GX, N_GY, 3, TX, TY, Z).transpose(2, 0, 3, 1, 4, 5).reshape(3, NX, NY, Z)
    return new_dual, site_shift, displacement
```

```python
import functools
import math

import jax
import jax.numpy as jnp
from jax import lax
from jax.experimental import pallas as pl
from jax.experimental.pallas import tpu as pltpu
from jax.sharding import PartitionSpec as P

TX = 4
TY = 4
Z = 256
SIDE = 2
BLOCK = 128
K_MAX = 12
SITES = K_MAX * BLOCK
INNER = SIDE * SIDE
HALF = 8

step_rate = 0.5
KAPPA = 2.0 / math.log(2.0)
SHIFT = 44.0
SCALE = 2.0**-20
NEVER = -1.0e7

FIELDS = 24
ROWS = 16
CHUNK = 64


def halves(values):
    high = values.astype(jnp.bfloat16)
    low = (values - high.astype(jnp.float32)).astype(jnp.bfloat16)
    return high, low


def both(values):
    high, low = halves(values)
    high = high.astype(jnp.float32)
    return jnp.concatenate([high, low.astype(jnp.float32)], 0).astype(jnp.bfloat16)


def along_sites(left, right):
    return lax.dot_general(
        left, right, (((1,), (1,)), ((), ())), preferred_element_type=jnp.float32
    )


def along_points(left, right):
    return jnp.dot(left, right, preferred_element_type=jnp.float32)


def joined(sums):
    return sums[:HALF] + sums[HALF : 2 * HALF]


def pass_kernel(moments, ids_ref, count_ref, table_ref, *refs):
    if moments:
        dual_ref, out_ref, disp_ref, site_ref, c_ref, d_ref = refs
    else:
        out_ref, site_ref, c_ref = refs
    count = count_ref[0]
    places = []
    for m in range(K_MAX):
        slot = ids_ref[m]
        row, col = slot // (3 * SIDE), slot % (3 * SIDE)
        tx, ty = row // SIDE, col // SIDE
        inner = row % SIDE * SIDE + col % SIDE
        places.append((tx, ty, inner))
        base = (ty * 3 + tx) * FIELDS + inner
        off_x = ((tx - 1) * TX).astype(jnp.float32)
        off_y = ((ty - 1) * TY).astype(jnp.float32)
        lanes = pl.ds(m * BLOCK, BLOCK)
        site_ref[0:1, lanes] = table_ref[pl.ds(base, 1), :] * TX + off_x
        site_ref[1:2, lanes] = table_ref[pl.ds(base + INNER, 1), :] * TY + off_y
        site_ref[2:3, lanes] = table_ref[pl.ds(base + 2 * INNER, 1), :] * Z
        if moments:
            weight = dual_ref[pl.ds(tx * ROWS + ty * INNER + inner, 1), :]
        else:
            weight = table_ref[pl.ds(base + 3 * INNER, 1), :]
        site_ref[3:4, lanes] = jnp.where(m < count, weight, NEVER)
    site_x, site_y, site_z = site_ref[0:1, :], site_ref[1:2, :], site_ref[2:3, :]
    rel_y = site_y - 2.0
    fixed = site_ref[3:4, :] - rel_y * rel_y
    for g in range(2):
        rel_x = site_x - (1.0 + 2.0 * g)
        site_ref[4 + g : 5 + g, :] = KAPPA * (fixed - rel_x * rel_x)

    def visit(chunk, carry):
        first = pl.multiple_of(chunk * CHUNK, CHUNK)
        rows = pl.ds(first, CHUNK)
        at_z = lax.broadcasted_iota(jnp.int32, (CHUNK, BLOCK), 0) + first
        at_z = at_z.astype(jnp.float32) + 0.5
        peaks = [None, None]
        for m in range(K_MAX):
            lanes = pl.ds(m * BLOCK, BLOCK)
            dz = at_z - site_ref[2:3, lanes]
            fall = dz * dz * -KAPPA
            for g in range(2):
                t = fall + site_ref[4 + g : 5 + g, lanes]
                peaks[g] = t if peaks[g] is None else jnp.maximum(peaks[g], t)
        tops = [jnp.max(p, axis=1, keepdims=True) - SHIFT for p in peaks]
        for m in range(K_MAX):
            lanes = pl.ds(m * BLOCK, BLOCK)
            dz = at_z - site_ref[2:3, lanes]
            fall = dz * dz * -KAPPA
            for g in range(2):
                t = fall + site_ref[4 + g : 5 + g, lanes]
                e = jnp.exp2(t - tops[g])
                c_ref[2 * g, rows, lanes], c_ref[2 * g + 1, rows, lanes] = halves(e)
                if moments:
                    d_ref[2 * g, rows, lanes], d_ref[2 * g + 1, rows, lanes] = halves(e * dz)
        return carry

    lax.fori_loop(0, Z // CHUNK, visit, 0)

    point = lax.broadcasted_iota(jnp.int32, (HALF, SITES), 0)
    at_y = (point % TY).astype(jnp.float32) + 0.5
    sums = [jnp.zeros((1, SITES), jnp.float32) for _ in range(4 if moments else 1)]
    for g in range(2):
        at_x = (point // TY).astype(jnp.float32) + (2.0 * g + 0.5)
        cross = (at_x - (1.0 + 2.0 * g)) * (site_x - (1.0 + 2.0 * g)) + (at_y - 2.0) * rel_y
        a = jnp.exp2((2.0 * KAPPA) * cross - SHIFT)
        c_high, c_low = c_ref[2 * g], c_ref[2 * g + 1]
        if moments:
            ax, ay = a * (at_x - site_x), a * (at_y - site_y)
            d_high, d_low = d_ref[2 * g], d_ref[2 * g + 1]
            a_pair = both(a)
            left = jnp.concatenate([a_pair, both(ax), both(ay)], 0)
            found = along_sites(left, c_high) + along_sites(left, c_low)
            share = 1.0 / joined(found)
            deep = along_sites(a_pair, d_high) + along_sites(a_pair, d_low)
            shown = (joined(found[2 * HALF :]), joined(found[4 * HALF :]), joined(deep))
            for c in range(3):
                value = -(shown[c] * share)
                disp_ref[c, 2 * g] = value[:TY]
                disp_ref[c, 2 * g + 1] = value[TY:]
        else:
            a_pair = both(a)
            share = 1.0 / joined(along_sites(a_pair, c_high) + along_sites(a_pair, c_low))
        pair = both(share * SCALE)
        back = joined(along_points(pair, c_high) + along_points(pair, c_low))
        weighted = [a * back]
        if moments:
            deep = joined(along_points(pair, d_high) + along_points(pair, d_low))
            weighted += [ax * back, ay * back, a * deep]
        for i, part in enumerate(weighted):
            sums[i] = sums[i] + jnp.sum(part, axis=0, keepdims=True)

    out_ref[...] = jnp.zeros_like(out_ref)
    for i, total in enumerate(sums):
        site_ref[i : i + 1, :] = total * (1.0 / SCALE)
    for m in range(K_MAX):
        tx, ty, inner = places[m]
        lanes = pl.ds(m * BLOCK, BLOCK)
        for i in range(len(sums)):
            if moments:
                to = (tx * 3 + ty) * (4 * INNER) + i * INNER + inner
            else:
                to = tx * ROWS + ty * INNER + inner
            out_ref[pl.ds(to, 1), :] = site_ref[i : i + 1, lanes]


def run_pass(ids, count, table, duals=None):
    moments = duals is not None
    smem = pl.BlockSpec(memory_space=pltpu.SMEM)
    vmem = pl.BlockSpec(memory_space=pltpu.VMEM)
    scratch = [
        pltpu.VMEM((8, SITES), jnp.float32),
        pltpu.VMEM((4, Z, SITES), jnp.bfloat16),
    ]
    if moments:
        shapes = (
            jax.ShapeDtypeStruct((9 * 4 * INNER, BLOCK), jnp.float32),
            jax.ShapeDtypeStruct((3, TX, TY, Z), jnp.float32),
        )
        specs, given = (vmem, vmem), (ids, count, table, duals)
        scratch.append(pltpu.VMEM((4, Z, SITES), jnp.bfloat16))
    else:
        shapes = jax.ShapeDtypeStruct((3 * ROWS, BLOCK), jnp.float32)
        specs, given = vmem, (ids, count, table)
    return pl.pallas_call(
        functools.partial(pass_kernel, moments),
        out_shape=shapes,
        in_specs=[smem, smem] + [vmem] * (len(given) - 2),
        out_specs=specs,
        scratch_shapes=scratch,
        compiler_params=pltpu.CompilerParams(vmem_limit_bytes=24 * 2**20),
    )(*given)


def moved(array, axis, by):
    peers = lax.axis_size(axis)
    return lax.ppermute(array, axis, [(i, (i + by) % peers) for i in range(peers)])


def with_sides(array, axis):
    return jnp.concatenate([moved(array, axis, 1), array, moved(array, axis, -1)], 0)


def folded(array, axis):
    third = array.shape[0] // 3
    below, own, above = array[:third], array[third : 2 * third], array[2 * third :]
    return own + moved(above, axis, 1) + moved(below, axis, -1)


def on_device(site_frac, dual_weight, target_mass, block_list, block_count):
    ids = block_list.reshape(K_MAX)
    count = block_count.reshape(1)
    weight = dual_weight.reshape(INNER, BLOCK)
    target = target_mass.reshape(INNER, BLOCK)
    tile = jnp.concatenate(
        [
            site_frac.reshape(3 * INNER, BLOCK),
            weight,
            target,
            jnp.zeros((FIELDS - 5 * INNER, BLOCK), jnp.float32),
        ],
        0,
    )
    table = with_sides(with_sides(tile, "gx"), "gy")

    mass = folded(run_pass(ids, count, table), "gx")
    below, own, above = (mass[i * INNER : (i + 1) * INNER] for i in range(3))
    lower = moved(mass[INNER : 3 * INNER], "gy", 1)
    upper = moved(mass[: 2 * INNER], "gy", -1)
    lowest = moved(above, "gy", 2)
    highest = moved(below, "gy", -2)
    totals = (
        lower[:INNER] + lowest + below,
        own + lower[INNER:] + upper[:INNER],
        upper[INNER:] + above + highest,
    )
    mids = []
    for ty in range(3):
        start = (ty * 3 + 1) * FIELDS
        old = table[start + 3 * INNER : start + 4 * INNER]
        goal = table[start + 4 * INNER : start + 5 * INNER]
        mids.append(old + step_rate * (goal - totals[ty]))
    column = jnp.concatenate([*mids, jnp.zeros((ROWS - 3 * INNER, BLOCK), jnp.float32)], 0)
    duals = with_sides(column, "gx")

    spread, displacement = run_pass(ids, count, table, duals)
    sums = folded(folded(spread, "gx"), "gy")
    mass = sums[:INNER]
    new_dual = mids[1] + step_rate * (target - mass)
    site_shift = sums[INNER:].reshape(3, INNER, BLOCK) / (mass + target)[None]
    return (
        new_dual.reshape(SIDE, SIDE, BLOCK),
        site_shift.reshape(3, SIDE, SIDE, BLOCK),
        displacement,
    )


def solution(mesh):
    in_specs = (
        P(None, "gx", "gy", None),
        P("gx", "gy", None),
        P("gx", "gy", None),
        P("gx", "gy", None),
        P("gx", "gy"),
    )
    out_specs = (P("gx", "gy", None), P(None, "gx", "gy", None), P(None, "gx", "gy", None))
    return jax.shard_map(
        on_device, mesh=mesh, in_specs=in_specs, out_specs=out_specs, check_vma=False
    )
```

```python
import functools
import math

import jax
import jax.numpy as jnp
from jax import lax
from jax.experimental import pallas as pl
from jax.experimental.pallas import tpu as pltpu
from jax.sharding import PartitionSpec as P

TX = 4
TY = 4
Z = 256
SIDE = 2
BLOCK = 128
K_MAX = 12
SITES = K_MAX * BLOCK
INNER = SIDE * SIDE
HALF = 8

step_rate = 0.5
KAPPA = 2.0 / math.log(2.0)
SHIFT = 44.0
SCALE = 2.0**-20
NEVER = -1.0e7

FIELDS = 24
ROWS = 16
CHUNK = 64


def halves(values):
    high = values.astype(jnp.bfloat16)
    low = (values - high.astype(jnp.float32)).astype(jnp.bfloat16)
    return high, low


def both(values):
    high, low = halves(values)
    high = high.astype(jnp.float32)
    return jnp.concatenate([high, low.astype(jnp.float32)], 0).astype(jnp.bfloat16)


def along_sites(left, right):
    return lax.dot_general(
        left, right, (((1,), (1,)), ((), ())), preferred_element_type=jnp.float32
    )


def along_points(left, right):
    return jnp.dot(left, right, preferred_element_type=jnp.float32)


def joined(sums):
    return sums[:HALF] + sums[HALF : 2 * HALF]


def pass_kernel(moments, ids_ref, table_ref, *refs):
    if moments:
        mass_ref, out_ref, disp_ref, site_ref, c_ref, d_ref = refs
    else:
        out_ref, site_ref, c_ref = refs
    count, way_x, way_y = (ids_ref[K_MAX + i] for i in range(3))
    places = []
    for m in range(K_MAX):
        slot = ids_ref[m]
        row, col = slot // (3 * SIDE), slot % (3 * SIDE)
        tx, ty = row // SIDE, col // SIDE
        inner = row % SIDE * SIDE + col % SIDE
        bx, by = 1 + (tx - 1) * way_x, 1 + (ty - 1) * way_y
        places.append((bx, by, inner))
        base = (by * 3 + bx) * FIELDS + inner
        off_x = ((tx - 1) * TX).astype(jnp.float32)
        off_y = ((ty - 1) * TY).astype(jnp.float32)
        lanes = pl.ds(m * BLOCK, BLOCK)
        site_ref[0:1, lanes] = table_ref[pl.ds(base, 1), :] * TX + off_x
        site_ref[1:2, lanes] = table_ref[pl.ds(base + INNER, 1), :] * TY + off_y
        site_ref[2:3, lanes] = table_ref[pl.ds(base + 2 * INNER, 1), :] * Z
        weight = table_ref[pl.ds(base + 3 * INNER, 1), :]
        if moments:
            goal = table_ref[pl.ds(base + 4 * INNER, 1), :]
            mass = mass_ref[pl.ds((by * 3 + bx) * INNER + inner, 1), :]
            weight = weight + step_rate * (goal - mass)
        site_ref[3:4, lanes] = jnp.where(m < count, weight, NEVER)
    site_x, site_y, site_z = site_ref[0:1, :], site_ref[1:2, :], site_ref[2:3, :]
    rel_y = site_y - 2.0
    fixed = site_ref[3:4, :] - rel_y * rel_y
    for g in range(2):
        rel_x = site_x - (1.0 + 2.0 * g)
        site_ref[4 + g : 5 + g, :] = KAPPA * (fixed - rel_x * rel_x)

    def visit(chunk, carry):
        first = pl.multiple_of(chunk * CHUNK, CHUNK)
        rows = pl.ds(first, CHUNK)
        at_z = lax.broadcasted_iota(jnp.int32, (CHUNK, BLOCK), 0) + first
        at_z = at_z.astype(jnp.float32) + 0.5
        peaks = [None, None]
        for m in range(K_MAX):
            lanes = pl.ds(m * BLOCK, BLOCK)
            dz = at_z - site_ref[2:3, lanes]
            fall = dz * dz * -KAPPA
            for g in range(2):
                t = fall + site_ref[4 + g : 5 + g, lanes]
                peaks[g] = t if peaks[g] is None else jnp.maximum(peaks[g], t)
        tops = [jnp.max(p, axis=1, keepdims=True) - SHIFT for p in peaks]
        for m in range(K_MAX):
            lanes = pl.ds(m * BLOCK, BLOCK)
            dz = at_z - site_ref[2:3, lanes]
            fall = dz * dz * -KAPPA
            for g in range(2):
                t = fall + site_ref[4 + g : 5 + g, lanes]
                e = jnp.exp2(t - tops[g])
                c_ref[2 * g, rows, lanes], c_ref[2 * g + 1, rows, lanes] = halves(e)
                if moments:
                    d_ref[2 * g, rows, lanes], d_ref[2 * g + 1, rows, lanes] = halves(e * dz)
        return carry

    lax.fori_loop(0, Z // CHUNK, visit, 0)

    point = lax.broadcasted_iota(jnp.int32, (HALF, SITES), 0)
    at_y = (point % TY).astype(jnp.float32) + 0.5
    sums = [jnp.zeros((1, SITES), jnp.float32) for _ in range(4 if moments else 1)]
    for g in range(2):
        at_x = (point // TY).astype(jnp.float32) + (2.0 * g + 0.5)
        cross = (at_x - (1.0 + 2.0 * g)) * (site_x - (1.0 + 2.0 * g)) + (at_y - 2.0) * rel_y
        a = jnp.exp2((2.0 * KAPPA) * cross - SHIFT)
        c_high, c_low = c_ref[2 * g], c_ref[2 * g + 1]
        if moments:
            ax, ay = a * (at_x - site_x), a * (at_y - site_y)
            d_high, d_low = d_ref[2 * g], d_ref[2 * g + 1]
            a_pair = both(a)
            left = jnp.concatenate([a_pair, both(ax), both(ay)], 0)
            found = along_sites(left, c_high) + along_sites(left, c_low)
            share = 1.0 / joined(found)
            deep = along_sites(a_pair, d_high) + along_sites(a_pair, d_low)
            shown = (joined(found[2 * HALF :]), joined(found[4 * HALF :]), joined(deep))
            for c in range(3):
                value = -(shown[c] * share)
                disp_ref[c, 2 * g] = value[:TY]
                disp_ref[c, 2 * g + 1] = value[TY:]
        else:
            a_pair = both(a)
            share = 1.0 / joined(along_sites(a_pair, c_high) + along_sites(a_pair, c_low))
        pair = both(share * SCALE)
        back = joined(along_points(pair, c_high) + along_points(pair, c_low))
        weighted = [a * back]
        if moments:
            deep = joined(along_points(pair, d_high) + along_points(pair, d_low))
            weighted += [ax * back, ay * back, a * deep]
        for i, part in enumerate(weighted):
            sums[i] = sums[i] + jnp.sum(part, axis=0, keepdims=True)

    out_ref[...] = jnp.zeros_like(out_ref)
    for i, total in enumerate(sums):
        site_ref[i : i + 1, :] = total * (1.0 / SCALE)
    for m in range(K_MAX):
        bx, by, inner = places[m]
        lanes = pl.ds(m * BLOCK, BLOCK)
        for i in range(len(sums)):
            if moments:
                to = (bx * 3 + by) * (4 * INNER) + i * INNER + inner
            else:
                to = bx * ROWS + by * INNER + inner
            out_ref[pl.ds(to, 1), :] = site_ref[i : i + 1, lanes]


def run_pass(ids, table, masses=None):
    moments = masses is not None
    smem = pl.BlockSpec(memory_space=pltpu.SMEM)
    vmem = pl.BlockSpec(memory_space=pltpu.VMEM)
    scratch = [
        pltpu.VMEM((8, SITES), jnp.float32),
        pltpu.VMEM((4, Z, SITES), jnp.bfloat16),
    ]
    if moments:
        shapes = (
            jax.ShapeDtypeStruct((9 * 4 * INNER, BLOCK), jnp.float32),
            jax.ShapeDtypeStruct((3, TX, TY, Z), jnp.float32),
        )
        specs, given = (vmem, vmem), (ids, table, masses)
        scratch.append(pltpu.VMEM((4, Z, SITES), jnp.bfloat16))
    else:
        shapes = jax.ShapeDtypeStruct((3 * ROWS, BLOCK), jnp.float32)
        specs, given = vmem, (ids, table)
    return pl.pallas_call(
        functools.partial(pass_kernel, moments),
        out_shape=shapes,
        in_specs=[smem] + [vmem] * (len(given) - 1),
        out_specs=specs,
        scratch_shapes=scratch,
        compiler_params=pltpu.CompilerParams(vmem_limit_bytes=24 * 2**20),
    )(*given)


def partner(kind, i, peers):
    if kind == "even":
        return i ^ 1
    if kind == "odd":
        return (i + 1 if i % 2 else i - 1) % peers
    if kind == "even2":
        return i ^ 2
    return (i + 2 if i % 4 >= 2 else i - 2) % peers


def swapped(array, axis, kind):
    peers = lax.axis_size(axis)
    return lax.ppermute(array, axis, [(i, partner(kind, i, peers)) for i in range(peers)])


def with_sides(array, axis):
    return jnp.concatenate([swapped(array, axis, "even"), array, swapped(array, axis, "odd")], 0)


def folded(array, axis):
    third = array.shape[0] // 3
    return (
        array[third : 2 * third]
        + swapped(array[:third], axis, "even")
        + swapped(array[2 * third :], axis, "odd")
    )


def folded_with_sides(blocks, axis):
    even, own, odd = blocks
    rows = own.shape[0]
    place = lax.axis_index(axis) % 4
    outer = (place == 0) | (place == 3)
    near_even = swapped(jnp.concatenate([own, even], 0), axis, "even")
    far_even = swapped(jnp.where(outer, even, odd), axis, "even2")
    near_odd = swapped(jnp.concatenate([own, odd], 0), axis, "odd")
    far_odd = swapped(jnp.where(outer, odd, even), axis, "odd2")
    return (
        near_even[:rows] + even + jnp.where(outer, far_even, far_odd),
        own + near_even[rows:] + near_odd[rows:],
        near_odd[:rows] + odd + jnp.where(outer, far_odd, far_even),
    )


def on_device(site_frac, dual_weight, target_mass, block_list, block_count):
    ways = [2 * (lax.axis_index(axis) % 2) - 1 for axis in ("gx", "gy")]
    ids = jnp.concatenate(
        [block_list.reshape(K_MAX), block_count.reshape(1), jnp.stack(ways).astype(jnp.int32)]
    )
    weight = dual_weight.reshape(INNER, BLOCK)
    target = target_mass.reshape(INNER, BLOCK)
    tile = jnp.concatenate(
        [
            site_frac.reshape(3 * INNER, BLOCK),
            weight,
            target,
            jnp.zeros((FIELDS - 5 * INNER, BLOCK), jnp.float32),
        ],
        0,
    )
    table = with_sides(with_sides(tile, "gx"), "gy")

    partial = run_pass(ids, table)
    blocks = folded_with_sides([partial[i * ROWS : i * ROWS + 3 * INNER] for i in range(3)], "gx")
    rims = [
        jnp.concatenate([b[j * INNER : (j + 1) * INNER] for b in blocks], 0) for j in range(3)
    ]
    masses = jnp.concatenate(folded_with_sides(rims, "gy"), 0)

    spread, displacement = run_pass(ids, table, masses)
    sums = folded(folded(spread, "gx"), "gy")
    mass = sums[:INNER]
    mid = weight + step_rate * (target - masses[4 * INNER : 5 * INNER])
    new_dual = mid + step_rate * (target - mass)
    site_shift = sums[INNER:].reshape(3, INNER, BLOCK) / (mass + target)[None]
    return (
        new_dual.reshape(SIDE, SIDE, BLOCK),
        site_shift.reshape(3, SIDE, SIDE, BLOCK),
        displacement,
    )


def solution(mesh):
    in_specs = (
        P(None, "gx", "gy", None),
        P("gx", "gy", None),
        P("gx", "gy", None),
        P("gx", "gy", None),
        P("gx", "gy"),
    )
    out_specs = (P("gx", "gy", None), P(None, "gx", "gy", None), P(None, "gx", "gy", None))
    return jax.shard_map(
        on_device, mesh=mesh, in_specs=in_specs, out_specs=out_specs, check_vma=False
    )
```

```python
import functools
import math

import jax
import jax.numpy as jnp
from jax import lax
from jax.experimental import pallas as pl
from jax.experimental.pallas import tpu as pltpu
from jax.sharding import PartitionSpec as P

TX = 4
TY = 4
Z = 256
SIDE = 2
BLOCK = 128
K_MAX = 12
SITES = K_MAX * BLOCK
INNER = SIDE * SIDE
HALF = 8

step_rate = 0.5
KAPPA = 2.0 / math.log(2.0)
SHIFT = 44.0
SCALE = 2.0**-20
NEVER = -1.0e7

FIELDS = 24
ROWS = 16
CHUNK = 64


def halves(values):
    high = values.astype(jnp.bfloat16)
    low = (values - high.astype(jnp.float32)).astype(jnp.bfloat16)
    return high, low


def both(values):
    high, low = halves(values)
    high = high.astype(jnp.float32)
    return jnp.concatenate([high, low.astype(jnp.float32)], 0).astype(jnp.bfloat16)


def along_sites(left, right):
    return lax.dot_general(
        right, left, (((1,), (1,)), ((), ())), preferred_element_type=jnp.float32
    ).T


def along_points(left, right):
    return jnp.dot(left, right, preferred_element_type=jnp.float32)


def joined(sums):
    return sums[:HALF] + sums[HALF : 2 * HALF]


def pass_kernel(moments, ids_ref, table_ref, *refs):
    if moments:
        mass_ref, out_ref, disp_ref, site_ref, c_ref, d_ref = refs
    else:
        out_ref, site_ref, c_ref = refs
    count, way_x, way_y = (ids_ref[K_MAX + i] for i in range(3))
    places = []
    for m in range(K_MAX):
        slot = ids_ref[m]
        row, col = slot // (3 * SIDE), slot % (3 * SIDE)
        tx, ty = row // SIDE, col // SIDE
        inner = row % SIDE * SIDE + col % SIDE
        bx, by = 1 + (tx - 1) * way_x, 1 + (ty - 1) * way_y
        places.append((bx, by, inner))
        base = (by * 3 + bx) * FIELDS + inner
        off_x = ((tx - 1) * TX).astype(jnp.float32)
        off_y = ((ty - 1) * TY).astype(jnp.float32)
        lanes = pl.ds(m * BLOCK, BLOCK)
        site_ref[0:1, lanes] = table_ref[pl.ds(base, 1), :] * TX + off_x
        site_ref[1:2, lanes] = table_ref[pl.ds(base + INNER, 1), :] * TY + off_y
        site_ref[2:3, lanes] = table_ref[pl.ds(base + 2 * INNER, 1), :] * Z
        weight = table_ref[pl.ds(base + 3 * INNER, 1), :]
        if moments:
            goal = table_ref[pl.ds(base + 4 * INNER, 1), :]
            mass = mass_ref[pl.ds((by * 3 + bx) * INNER + inner, 1), :]
            weight = weight + step_rate * (goal - mass)
        site_ref[3:4, lanes] = jnp.where(m < count, weight, NEVER)
    site_x, site_y, site_z = site_ref[0:1, :], site_ref[1:2, :], site_ref[2:3, :]
    rel_y = site_y - 2.0
    fixed = site_ref[3:4, :] - rel_y * rel_y
    for g in range(2):
        rel_x = site_x - (1.0 + 2.0 * g)
        site_ref[4 + g : 5 + g, :] = KAPPA * (fixed - rel_x * rel_x)

    def visit(chunk, carry):
        first = pl.multiple_of(chunk * CHUNK, CHUNK)
        rows = pl.ds(first, CHUNK)
        at_z = lax.broadcasted_iota(jnp.int32, (CHUNK, BLOCK), 0) + first
        at_z = at_z.astype(jnp.float32) + 0.5
        peaks = [None, None]
        for m in range(K_MAX):
            lanes = pl.ds(m * BLOCK, BLOCK)
            dz = at_z - site_ref[2:3, lanes]
            fall = dz * dz * -KAPPA
            for g in range(2):
                t = fall + site_ref[4 + g : 5 + g, lanes]
                peaks[g] = t if peaks[g] is None else jnp.maximum(peaks[g], t)
        tops = [jnp.max(p, axis=1, keepdims=True) - SHIFT for p in peaks]
        for m in range(K_MAX):
            lanes = pl.ds(m * BLOCK, BLOCK)
            dz = at_z - site_ref[2:3, lanes]
            fall = dz * dz * -KAPPA
            for g in range(2):
                t = fall + site_ref[4 + g : 5 + g, lanes]
                e = jnp.exp2(t - tops[g])
                c_ref[2 * g, rows, lanes], c_ref[2 * g + 1, rows, lanes] = halves(e)
                if moments:
                    d_ref[2 * g, rows, lanes], d_ref[2 * g + 1, rows, lanes] = halves(e * dz)
        return carry

    lax.fori_loop(0, Z // CHUNK, visit, 0, unroll=True)

    point = lax.broadcasted_iota(jnp.int32, (HALF, SITES), 0)
    at_y = (point % TY).astype(jnp.float32) + 0.5
    sums = [jnp.zeros((1, SITES), jnp.float32) for _ in range(4 if moments else 1)]
    for g in range(2):
        at_x = (point // TY).astype(jnp.float32) + (2.0 * g + 0.5)
        cross = (at_x - (1.0 + 2.0 * g)) * (site_x - (1.0 + 2.0 * g)) + (at_y - 2.0) * rel_y
        a = jnp.exp2((2.0 * KAPPA) * cross - SHIFT)
        c_high, c_low = c_ref[2 * g], c_ref[2 * g + 1]
        if moments:
            ax, ay = a * (at_x - site_x), a * (at_y - site_y)
            d_high, d_low = d_ref[2 * g], d_ref[2 * g + 1]
            a_pair = both(a)
            left = jnp.concatenate([a_pair, both(ax), both(ay)], 0)
            found = along_sites(left, c_high) + along_sites(left, c_low)
            share = 1.0 / joined(found)
            deep = along_sites(a_pair, d_high) + along_sites(a_pair, d_low)
            shown = (joined(found[2 * HALF :]), joined(found[4 * HALF :]), joined(deep))
            for c in range(3):
                value = -(shown[c] * share)
                disp_ref[c, 2 * g] = value[:TY]
                disp_ref[c, 2 * g + 1] = value[TY:]
        else:
            a_pair = both(a)
            share = 1.0 / joined(along_sites(a_pair, c_high) + along_sites(a_pair, c_low))
        pair = both(share * SCALE)
        back = joined(along_points(pair, c_high) + along_points(pair, c_low))
        weighted = [a * back]
        if moments:
            deep = joined(along_points(pair, d_high) + along_points(pair, d_low))
            weighted += [ax * back, ay * back, a * deep]
        for i, part in enumerate(weighted):
            sums[i] = sums[i] + jnp.sum(part, axis=0, keepdims=True)

    out_ref[...] = jnp.zeros_like(out_ref)
    for i, total in enumerate(sums):
        site_ref[i : i + 1, :] = total * (1.0 / SCALE)
    for m in range(K_MAX):
        bx, by, inner = places[m]
        lanes = pl.ds(m * BLOCK, BLOCK)
        for i in range(len(sums)):
            if moments:
                to = (bx * 3 + by) * (4 * INNER) + i * INNER + inner
            else:
                to = bx * ROWS + by * INNER + inner
            out_ref[pl.ds(to, 1), :] = site_ref[i : i + 1, lanes]


def run_pass(ids, table, masses=None):
    moments = masses is not None
    smem = pl.BlockSpec(memory_space=pltpu.SMEM)
    vmem = pl.BlockSpec(memory_space=pltpu.VMEM)
    scratch = [
        pltpu.VMEM((8, SITES), jnp.float32),
        pltpu.VMEM((4, Z, SITES), jnp.bfloat16),
    ]
    if moments:
        shapes = (
            jax.ShapeDtypeStruct((9 * 4 * INNER, BLOCK), jnp.float32),
            jax.ShapeDtypeStruct((3, TX, TY, Z), jnp.float32),
        )
        specs, given = (vmem, vmem), (ids, table, masses)
        scratch.append(pltpu.VMEM((4, Z, SITES), jnp.bfloat16))
    else:
        shapes = jax.ShapeDtypeStruct((3 * ROWS, BLOCK), jnp.float32)
        specs, given = vmem, (ids, table)
    return pl.pallas_call(
        functools.partial(pass_kernel, moments),
        out_shape=shapes,
        in_specs=[smem] + [vmem] * (len(given) - 1),
        out_specs=specs,
        scratch_shapes=scratch,
        compiler_params=pltpu.CompilerParams(vmem_limit_bytes=24 * 2**20),
    )(*given)


def pack_kernel(frac_ref, weight_ref, target_ref, out_ref):
    for x in range(SIDE):
        for c in range(3):
            out_ref[pl.ds(c * INNER + x * SIDE, SIDE), :] = frac_ref[c, x]
        out_ref[pl.ds(3 * INNER + x * SIDE, SIDE), :] = weight_ref[x]
        out_ref[pl.ds(4 * INNER + x * SIDE, SIDE), :] = target_ref[x]
    out_ref[pl.ds(5 * INNER, FIELDS - 5 * INNER), :] = jnp.zeros((FIELDS - 5 * INNER, BLOCK), jnp.float32)


def finish_kernel(tile_ref, masses_ref, own_ref, even_ref, odd_ref, dual_ref, shift_ref):
    sums = own_ref[4 * INNER : 8 * INNER] + even_ref[...] + odd_ref[...]
    weight, target = tile_ref[3 * INNER : 4 * INNER], tile_ref[4 * INNER : 5 * INNER]
    mid = weight + step_rate * (target - masses_ref[4 * INNER : 5 * INNER])
    dual = mid + step_rate * (target - sums[:INNER])
    share = sums[:INNER] + target
    for x in range(SIDE):
        rows = slice(x * SIDE, (x + 1) * SIDE)
        dual_ref[x] = dual[rows]
        for c in range(3):
            moment = sums[(c + 1) * INNER : (c + 2) * INNER]
            shift_ref[c, x] = (moment / share)[rows]


def run_small(kernel, shapes, *given):
    vmem = pl.BlockSpec(memory_space=pltpu.VMEM)
    shapes = jax.tree.map(lambda shape: jax.ShapeDtypeStruct(shape, jnp.float32), shapes, is_leaf=lambda s: type(s[0]) is int)
    return pl.pallas_call(
        kernel,
        out_shape=shapes,
        in_specs=[vmem] * len(given),
        out_specs=jax.tree.map(lambda _: vmem, shapes),
        compiler_params=pltpu.CompilerParams(vmem_limit_bytes=4 * 2**20),
    )(*given)


def partner(kind, i, peers):
    if kind == "even":
        return i ^ 1
    if kind == "odd":
        return (i + 1 if i % 2 else i - 1) % peers
    if kind == "even2":
        return i ^ 2
    return (i + 2 if i % 4 >= 2 else i - 2) % peers


def swapped(array, axis, kind):
    peers = lax.axis_size(axis)
    return lax.ppermute(array, axis, [(i, partner(kind, i, peers)) for i in range(peers)])


def with_sides(array, axis):
    return jnp.concatenate([swapped(array, axis, "even"), array, swapped(array, axis, "odd")], 0)


def folded(array, axis):
    third = array.shape[0] // 3
    return (
        array[third : 2 * third]
        + swapped(array[:third], axis, "even")
        + swapped(array[2 * third :], axis, "odd")
    )


def folded_with_sides(blocks, axis):
    even, own, odd = blocks
    rows = own.shape[0]
    place = lax.axis_index(axis) % 4
    outer = (place == 0) | (place == 3)
    near_even = swapped(jnp.concatenate([own, even], 0), axis, "even")
    far_even = swapped(jnp.where(outer, even, odd), axis, "even2")
    near_odd = swapped(jnp.concatenate([own, odd], 0), axis, "odd")
    far_odd = swapped(jnp.where(outer, odd, even), axis, "odd2")
    return (
        near_even[:rows] + even + jnp.where(outer, far_even, far_odd),
        own + near_even[rows:] + near_odd[rows:],
        near_odd[:rows] + odd + jnp.where(outer, far_odd, far_even),
    )


def on_device(site_frac, dual_weight, target_mass, block_list, block_count):
    ways = [2 * (lax.axis_index(axis) % 2) - 1 for axis in ("gx", "gy")]
    ids = jnp.concatenate(
        [block_list.reshape(K_MAX), block_count.reshape(1), jnp.stack(ways).astype(jnp.int32)]
    )
    tile = run_small(pack_kernel, (FIELDS, BLOCK), site_frac, dual_weight, target_mass)
    table = with_sides(with_sides(tile, "gx"), "gy")

    partial = run_pass(ids, table)
    blocks = folded_with_sides([partial[i * ROWS : i * ROWS + 3 * INNER] for i in range(3)], "gx")
    rims = [
        jnp.concatenate([b[j * INNER : (j + 1) * INNER] for b in blocks], 0) for j in range(3)
    ]
    masses = jnp.concatenate(folded_with_sides(rims, "gy"), 0)

    spread, displacement = run_pass(ids, table, masses)
    column = folded(spread, "gx")
    even = swapped(column[: 4 * INNER], "gy", "even")
    odd = swapped(column[8 * INNER :], "gy", "odd")
    new_dual, site_shift = run_small(
        finish_kernel, (dual_weight.shape, site_frac.shape), tile, masses, column, even, odd
    )
    return new_dual, site_shift, displacement


def solution(mesh):
    in_specs = (
        P(None, "gx", "gy", None),
        P("gx", "gy", None),
        P("gx", "gy", None),
        P("gx", "gy", None),
        P("gx", "gy"),
    )
    out_specs = (P("gx", "gy", None), P(None, "gx", "gy", None), P(None, "gx", "gy", None))
    return jax.shard_map(
        on_device, mesh=mesh, in_specs=in_specs, out_specs=out_specs, check_vma=False
    )
```

```python
import functools
import math

import jax
import jax.numpy as jnp
from jax import lax
from jax.experimental import pallas as pl
from jax.experimental.pallas import tpu as pltpu
from jax.sharding import PartitionSpec as P

TX = 4
TY = 4
Z = 256
SIDE = 2
BLOCK = 128
K_MAX = 12
SITES = K_MAX * BLOCK
INNER = SIDE * SIDE
HALF = 8

step_rate = 0.5
KAPPA = 2.0 / math.log(2.0)
SHIFT = 44.0
SCALE = 2.0**-20
NEVER = -1.0e7

FIELDS = 5
ROWS = 16
CHUNK = 64


def halves(values):
    high = values.astype(jnp.bfloat16)
    low = (values - high.astype(jnp.float32)).astype(jnp.bfloat16)
    return high, low


def both(values):
    high, low = halves(values)
    high = high.astype(jnp.float32)
    return jnp.concatenate([high, low.astype(jnp.float32)], 0).astype(jnp.bfloat16)


def along_sites(left, right):
    return lax.dot_general(
        right, left, (((1,), (1,)), ((), ())), preferred_element_type=jnp.float32
    ).T


def along_points(left, right):
    return jnp.dot(left, right, preferred_element_type=jnp.float32)


def joined(sums):
    return sums[:HALF] + sums[HALF : 2 * HALF]


def pass_kernel(moments, ids_ref, table_ref, *refs):
    if moments:
        mass_ref, out_ref, disp_ref, site_ref, c_ref, d_ref = refs
    else:
        out_ref, site_ref, c_ref = refs
    count, way_x, way_y = (ids_ref[K_MAX + i] for i in range(3))
    places = []
    for m in range(K_MAX):
        slot = ids_ref[m]
        row, col = slot // (3 * SIDE), slot % (3 * SIDE)
        tx, ty = row // SIDE, col // SIDE
        place_x, place_y = row % SIDE, col % SIDE
        inner = place_x * SIDE + place_y
        bx, by = 1 + (tx - 1) * way_x, 1 + (ty - 1) * way_y
        places.append((bx, by, inner))
        base = (by * 3 + bx) * FIELDS

        def field(f):
            return table_ref[base + f, place_x, pl.ds(place_y, 1), :]

        off_x = ((tx - 1) * TX).astype(jnp.float32)
        off_y = ((ty - 1) * TY).astype(jnp.float32)
        lanes = pl.ds(m * BLOCK, BLOCK)
        site_ref[0:1, lanes] = field(0) * TX + off_x
        site_ref[1:2, lanes] = field(1) * TY + off_y
        site_ref[2:3, lanes] = field(2) * Z
        weight = field(3)
        if moments:
            goal = field(4)
            mass = mass_ref[pl.ds((by * 3 + bx) * INNER + inner, 1), :]
            weight = weight + step_rate * (goal - mass)
        site_ref[3:4, lanes] = jnp.where(m < count, weight, NEVER)
    site_x, site_y, site_z = site_ref[0:1, :], site_ref[1:2, :], site_ref[2:3, :]
    rel_y = site_y - 2.0
    fixed = site_ref[3:4, :] - rel_y * rel_y
    for g in range(2):
        rel_x = site_x - (1.0 + 2.0 * g)
        site_ref[4 + g : 5 + g, :] = KAPPA * (fixed - rel_x * rel_x)

    def visit(chunk, carry):
        first = pl.multiple_of(chunk * CHUNK, CHUNK)
        rows = pl.ds(first, CHUNK)
        at_z = lax.broadcasted_iota(jnp.int32, (CHUNK, BLOCK), 0) + first
        at_z = at_z.astype(jnp.float32) + 0.5
        peaks = [None, None]
        for m in range(K_MAX):
            lanes = pl.ds(m * BLOCK, BLOCK)
            dz = at_z - site_ref[2:3, lanes]
            fall = dz * dz * -KAPPA
            for g in range(2):
                t = fall + site_ref[4 + g : 5 + g, lanes]
                peaks[g] = t if peaks[g] is None else jnp.maximum(peaks[g], t)
        tops = [jnp.max(p, axis=1, keepdims=True) - SHIFT for p in peaks]
        for m in range(K_MAX):
            lanes = pl.ds(m * BLOCK, BLOCK)
            dz = at_z - site_ref[2:3, lanes]
            fall = dz * dz * -KAPPA
            for g in range(2):
                t = fall + site_ref[4 + g : 5 + g, lanes]
                e = jnp.exp2(t - tops[g])
                c_ref[2 * g, rows, lanes], c_ref[2 * g + 1, rows, lanes] = halves(e)
                if moments:
                    d_ref[2 * g, rows, lanes], d_ref[2 * g + 1, rows, lanes] = halves(e * dz)
        return carry

    lax.fori_loop(0, Z // CHUNK, visit, 0, unroll=True)

    point = lax.broadcasted_iota(jnp.int32, (HALF, SITES), 0)
    at_y = (point % TY).astype(jnp.float32) + 0.5
    sums = [jnp.zeros((1, SITES), jnp.float32) for _ in range(4 if moments else 1)]
    for g in range(2):
        at_x = (point // TY).astype(jnp.float32) + (2.0 * g + 0.5)
        cross = (at_x - (1.0 + 2.0 * g)) * (site_x - (1.0 + 2.0 * g)) + (at_y - 2.0) * rel_y
        a = jnp.exp2((2.0 * KAPPA) * cross - SHIFT)
        c_high, c_low = c_ref[2 * g], c_ref[2 * g + 1]
        if moments:
            ax, ay = a * (at_x - site_x), a * (at_y - site_y)
            d_high, d_low = d_ref[2 * g], d_ref[2 * g + 1]
            a_pair = both(a)
            left = jnp.concatenate([a_pair, both(ax), both(ay)], 0)
            found = along_sites(left, c_high) + along_sites(left, c_low)
            share = 1.0 / joined(found)
            deep = along_sites(a_pair, d_high) + along_sites(a_pair, d_low)
            shown = (joined(found[2 * HALF :]), joined(found[4 * HALF :]), joined(deep))
            for c in range(3):
                value = -(shown[c] * share)
                disp_ref[c, 2 * g] = value[:TY]
                disp_ref[c, 2 * g + 1] = value[TY:]
        else:
            a_pair = both(a)
            share = 1.0 / joined(along_sites(a_pair, c_high) + along_sites(a_pair, c_low))
        pair = both(share * SCALE)
        back = joined(along_points(pair, c_high) + along_points(pair, c_low))
        weighted = [a * back]
        if moments:
            deep = joined(along_points(pair, d_high) + along_points(pair, d_low))
            weighted += [ax * back, ay * back, a * deep]
        for i, part in enumerate(weighted):
            sums[i] = sums[i] + jnp.sum(part, axis=0, keepdims=True)

    out_ref[...] = jnp.zeros_like(out_ref)
    for i, total in enumerate(sums):
        site_ref[i : i + 1, :] = total * (1.0 / SCALE)
    for m in range(K_MAX):
        bx, by, inner = places[m]
        lanes = pl.ds(m * BLOCK, BLOCK)
        for i in range(len(sums)):
            if moments:
                to = (bx * 3 + by) * (4 * INNER) + i * INNER + inner
            else:
                to = bx * ROWS + by * INNER + inner
            out_ref[pl.ds(to, 1), :] = site_ref[i : i + 1, lanes]


def run_pass(ids, table, masses=None):
    moments = masses is not None
    smem = pl.BlockSpec(memory_space=pltpu.SMEM)
    vmem = pl.BlockSpec(memory_space=pltpu.VMEM)
    scratch = [
        pltpu.VMEM((8, SITES), jnp.float32),
        pltpu.VMEM((4, Z, SITES), jnp.bfloat16),
    ]
    if moments:
        shapes = (
            jax.ShapeDtypeStruct((9 * 4 * INNER, BLOCK), jnp.float32),
            jax.ShapeDtypeStruct((3, TX, TY, Z), jnp.float32),
        )
        specs, given = (vmem, vmem), (ids, table, masses)
        scratch.append(pltpu.VMEM((4, Z, SITES), jnp.bfloat16))
    else:
        shapes = jax.ShapeDtypeStruct((3 * ROWS, BLOCK), jnp.float32)
        specs, given = vmem, (ids, table)
    return pl.pallas_call(
        functools.partial(pass_kernel, moments),
        out_shape=shapes,
        in_specs=[smem] + [vmem] * (len(given) - 1),
        out_specs=specs,
        scratch_shapes=scratch,
        compiler_params=pltpu.CompilerParams(vmem_limit_bytes=24 * 2**20),
    )(*given)


def finish_kernel(tile_ref, masses_ref, own_ref, even_ref, odd_ref, dual_ref, shift_ref):
    sums = own_ref[4 * INNER : 8 * INNER] + even_ref[...] + odd_ref[...]
    for x in range(SIDE):
        rows = slice(x * SIDE, (x + 1) * SIDE)
        mass, target = sums[rows], tile_ref[4, x]
        first = masses_ref[4 * INNER + x * SIDE : 4 * INNER + (x + 1) * SIDE]
        mid = tile_ref[3, x] + step_rate * (target - first)
        dual_ref[x] = mid + step_rate * (target - mass)
        for c in range(3):
            moment = sums[(c + 1) * INNER : (c + 2) * INNER]
            shift_ref[c, x] = moment[rows] / (mass + target)


def run_finish(like_dual, like_shift, *given):
    vmem = pl.BlockSpec(memory_space=pltpu.VMEM)
    return pl.pallas_call(
        finish_kernel,
        out_shape=tuple(jax.ShapeDtypeStruct(a.shape, jnp.float32) for a in (like_dual, like_shift)),
        in_specs=[vmem] * len(given),
        out_specs=(vmem, vmem),
        compiler_params=pltpu.CompilerParams(vmem_limit_bytes=4 * 2**20),
    )(*given)


def partner(kind, i, peers):
    if kind == "even":
        return i ^ 1
    if kind == "odd":
        return (i + 1 if i % 2 else i - 1) % peers
    if kind == "even2":
        return i ^ 2
    return (i + 2 if i % 4 >= 2 else i - 2) % peers


def swapped(array, axis, kind):
    peers = lax.axis_size(axis)
    return lax.ppermute(array, axis, [(i, partner(kind, i, peers)) for i in range(peers)])


def with_sides(array, axis):
    return jnp.concatenate([swapped(array, axis, "even"), array, swapped(array, axis, "odd")], 0)


def folded(array, axis):
    third = array.shape[0] // 3
    return (
        array[third : 2 * third]
        + swapped(array[:third], axis, "even")
        + swapped(array[2 * third :], axis, "odd")
    )


def folded_with_sides(blocks, axis):
    even, own, odd = blocks
    rows = own.shape[0]
    place = lax.axis_index(axis) % 4
    outer = (place == 0) | (place == 3)
    near_even = swapped(jnp.concatenate([own, even], 0), axis, "even")
    far_even = swapped(jnp.where(outer, even, odd), axis, "even2")
    near_odd = swapped(jnp.concatenate([own, odd], 0), axis, "odd")
    far_odd = swapped(jnp.where(outer, odd, even), axis, "odd2")
    return (
        near_even[:rows] + even + jnp.where(outer, far_even, far_odd),
        own + near_even[rows:] + near_odd[rows:],
        near_odd[:rows] + odd + jnp.where(outer, far_odd, far_even),
    )


def on_device(site_frac, dual_weight, target_mass, block_list, block_count):
    ways = [2 * (lax.axis_index(axis) % 2) - 1 for axis in ("gx", "gy")]
    ids = jnp.concatenate(
        [block_list.reshape(K_MAX), block_count.reshape(1), jnp.stack(ways).astype(jnp.int32)]
    )
    tile = lax.optimization_barrier(
        jnp.concatenate([site_frac, dual_weight[None], target_mass[None]], 0)
    )
    column, ids = lax.optimization_barrier((with_sides(tile, "gx"), ids))
    table = with_sides(column, "gy")

    partial = run_pass(ids, table)
    blocks = folded_with_sides([partial[i * ROWS : i * ROWS + 3 * INNER] for i in range(3)], "gx")
    rims = [
        jnp.concatenate([b[j * INNER : (j + 1) * INNER] for b in blocks], 0) for j in range(3)
    ]
    masses = jnp.concatenate(folded_with_sides(rims, "gy"), 0)

    spread, displacement = run_pass(ids, table, masses)
    summed = folded(spread, "gx")
    even = swapped(summed[: 4 * INNER], "gy", "even")
    odd = swapped(summed[8 * INNER :], "gy", "odd")
    new_dual, site_shift = run_finish(
        dual_weight, site_frac, tile, masses, summed, even, odd
    )
    return new_dual, site_shift, displacement


def solution(mesh):
    in_specs = (
        P(None, "gx", "gy", None),
        P("gx", "gy", None),
        P("gx", "gy", None),
        P("gx", "gy", None),
        P("gx", "gy"),
    )
    out_specs = (P("gx", "gy", None), P(None, "gx", "gy", None), P(None, "gx", "gy", None))
    return jax.shard_map(
        on_device, mesh=mesh, in_specs=in_specs, out_specs=out_specs, check_vma=False
    )
```

```python
import functools
import math

import jax
import jax.numpy as jnp
from jax import lax
from jax.experimental import pallas as pl
from jax.experimental.pallas import tpu as pltpu
from jax.sharding import PartitionSpec as P

TX = 4
TY = 4
Z = 256
SIDE = 2
BLOCK = 128
K_MAX = 12
SITES = K_MAX * BLOCK
INNER = SIDE * SIDE
HALF = 8

step_rate = 0.5
KAPPA = 2.0 / math.log(2.0)
SHIFT = 44.0
SCALE = 2.0**-20
NEVER = -1.0e7

FIELDS = 5
ROWS = 16
CHUNK = 64


def halves(values):
    high = values.astype(jnp.bfloat16)
    low = (values - high.astype(jnp.float32)).astype(jnp.bfloat16)
    return high, low


def both(values):
    high, low = halves(values)
    high = high.astype(jnp.float32)
    return jnp.concatenate([high, low.astype(jnp.float32)], 0).astype(jnp.bfloat16)


def along_sites(left, right):
    return lax.dot_general(
        right, left, (((1,), (1,)), ((), ())), preferred_element_type=jnp.float32
    ).T


def along_points(left, right):
    return jnp.dot(left, right, preferred_element_type=jnp.float32)


def joined(sums):
    return sums[:HALF] + sums[HALF : 2 * HALF]


def pass_kernel(moments, ids_ref, table_ref, *refs):
    if moments:
        mass_ref, out_ref, disp_ref, site_ref, c_ref, d_ref = refs
    else:
        out_ref, site_ref, c_ref = refs
    count, way_x, way_y = (ids_ref[K_MAX + i] for i in range(3))
    places = []
    for m in range(K_MAX):
        slot = ids_ref[m]
        row, col = slot // (3 * SIDE), slot % (3 * SIDE)
        tx, ty = row // SIDE, col // SIDE
        place_x, place_y = row % SIDE, col % SIDE
        inner = place_x * SIDE + place_y
        bx, by = 1 + (tx - 1) * way_x, 1 + (ty - 1) * way_y
        places.append((bx, by, inner))
        base = (by * 3 + bx) * FIELDS

        def field(f):
            return table_ref[base + f, place_x, pl.ds(place_y, 1), :]

        off_x = ((tx - 1) * TX).astype(jnp.float32)
        off_y = ((ty - 1) * TY).astype(jnp.float32)
        lanes = pl.ds(m * BLOCK, BLOCK)
        site_ref[0:1, lanes] = field(0) * TX + off_x
        site_ref[1:2, lanes] = field(1) * TY + off_y
        site_ref[2:3, lanes] = field(2) * Z
        weight = field(3)
        if moments:
            goal = field(4)
            mass = mass_ref[pl.ds((by * 3 + bx) * INNER + inner, 1), :]
            weight = weight + step_rate * (goal - mass)
        site_ref[3:4, lanes] = jnp.where(m < count, weight, NEVER)
    site_x, site_y, site_z = site_ref[0:1, :], site_ref[1:2, :], site_ref[2:3, :]
    rel_y = site_y - 2.0
    fixed = site_ref[3:4, :] - rel_y * rel_y
    for g in range(2):
        rel_x = site_x - (1.0 + 2.0 * g)
        site_ref[4 + g : 5 + g, :] = KAPPA * (fixed - rel_x * rel_x)

    def visit(chunk, carry):
        first = pl.multiple_of(chunk * CHUNK, CHUNK)
        rows = pl.ds(first, CHUNK)
        at_z = lax.broadcasted_iota(jnp.int32, (CHUNK, BLOCK), 0) + first
        at_z = at_z.astype(jnp.float32) + 0.5
        peaks, kept = [None, None], []
        for m in range(K_MAX):
            lanes = pl.ds(m * BLOCK, BLOCK)
            dz = at_z - site_ref[2:3, lanes]
            fall = dz * dz * -KAPPA
            for g in range(2):
                t = fall + site_ref[4 + g : 5 + g, lanes]
                kept.append(t)
                peaks[g] = t if peaks[g] is None else jnp.maximum(peaks[g], t)
        tops = [jnp.max(p, axis=1, keepdims=True) - SHIFT for p in peaks]
        for m in range(K_MAX):
            lanes = pl.ds(m * BLOCK, BLOCK)
            dz = at_z - site_ref[2:3, lanes]
            for g in range(2):
                e = jnp.exp2(kept[2 * m + g] - tops[g])
                c_ref[2 * g, rows, lanes], c_ref[2 * g + 1, rows, lanes] = halves(e)
                if moments:
                    d_ref[2 * g, rows, lanes], d_ref[2 * g + 1, rows, lanes] = halves(e * dz)
        return carry

    lax.fori_loop(0, Z // CHUNK, visit, 0, unroll=True)

    point = lax.broadcasted_iota(jnp.int32, (HALF, SITES), 0)
    at_y = (point % TY).astype(jnp.float32) + 0.5
    sums = [jnp.zeros((1, SITES), jnp.float32) for _ in range(4 if moments else 1)]
    for g in range(2):
        at_x = (point // TY).astype(jnp.float32) + (2.0 * g + 0.5)
        cross = (at_x - (1.0 + 2.0 * g)) * (site_x - (1.0 + 2.0 * g)) + (at_y - 2.0) * rel_y
        a = jnp.exp2((2.0 * KAPPA) * cross - SHIFT)
        c_high, c_low = c_ref[2 * g], c_ref[2 * g + 1]
        if moments:
            ax, ay = a * (at_x - site_x), a * (at_y - site_y)
            d_high, d_low = d_ref[2 * g], d_ref[2 * g + 1]
            a_pair = both(a)
            left = jnp.concatenate([a_pair, both(ax), both(ay)], 0)
            found = along_sites(left, c_high) + along_sites(left, c_low)
            share = 1.0 / joined(found)
            deep = along_sites(a_pair, d_high) + along_sites(a_pair, d_low)
            shown = (joined(found[2 * HALF :]), joined(found[4 * HALF :]), joined(deep))
            for c in range(3):
                value = -(shown[c] * share)
                disp_ref[c, 2 * g] = value[:TY]
                disp_ref[c, 2 * g + 1] = value[TY:]
        else:
            a_pair = both(a)
            share = 1.0 / joined(along_sites(a_pair, c_high) + along_sites(a_pair, c_low))
        pair = both(share * SCALE)
        back = joined(along_points(pair, c_high) + along_points(pair, c_low))
        weighted = [a * back]
        if moments:
            deep = joined(along_points(pair, d_high) + along_points(pair, d_low))
            weighted += [ax * back, ay * back, a * deep]
        for i, part in enumerate(weighted):
            sums[i] = sums[i] + jnp.sum(part, axis=0, keepdims=True)

    out_ref[...] = jnp.zeros_like(out_ref)
    for i, total in enumerate(sums):
        site_ref[i : i + 1, :] = total * (1.0 / SCALE)
    for m in range(K_MAX):
        bx, by, inner = places[m]
        lanes = pl.ds(m * BLOCK, BLOCK)
        for i in range(len(sums)):
            if moments:
                to = (bx * 3 + by) * (4 * INNER) + i * INNER + inner
            else:
                to = bx * ROWS + by * INNER + inner
            out_ref[pl.ds(to, 1), :] = site_ref[i : i + 1, lanes]


def run_pass(ids, table, masses=None):
    moments = masses is not None
    smem = pl.BlockSpec(memory_space=pltpu.SMEM)
    vmem = pl.BlockSpec(memory_space=pltpu.VMEM)
    scratch = [
        pltpu.VMEM((8, SITES), jnp.float32),
        pltpu.VMEM((4, Z, SITES), jnp.bfloat16),
    ]
    if moments:
        shapes = (
            jax.ShapeDtypeStruct((9 * 4 * INNER, BLOCK), jnp.float32),
            jax.ShapeDtypeStruct((3, TX, TY, Z), jnp.float32),
        )
        specs, given = (vmem, vmem), (ids, table, masses)
        scratch.append(pltpu.VMEM((4, Z, SITES), jnp.bfloat16))
    else:
        shapes = jax.ShapeDtypeStruct((3 * ROWS, BLOCK), jnp.float32)
        specs, given = vmem, (ids, table)
    return pl.pallas_call(
        functools.partial(pass_kernel, moments),
        out_shape=shapes,
        in_specs=[smem] + [vmem] * (len(given) - 1),
        out_specs=specs,
        scratch_shapes=scratch,
        compiler_params=pltpu.CompilerParams(vmem_limit_bytes=24 * 2**20),
    )(*given)


def finish_kernel(tile_ref, masses_ref, own_ref, even_ref, odd_ref, dual_ref, shift_ref):
    sums = own_ref[4 * INNER : 8 * INNER] + even_ref[...] + odd_ref[...]
    for x in range(SIDE):
        rows = slice(x * SIDE, (x + 1) * SIDE)
        mass, target = sums[rows], tile_ref[4, x]
        first = masses_ref[4 * INNER + x * SIDE : 4 * INNER + (x + 1) * SIDE]
        mid = tile_ref[3, x] + step_rate * (target - first)
        dual_ref[x] = mid + step_rate * (target - mass)
        for c in range(3):
            moment = sums[(c + 1) * INNER : (c + 2) * INNER]
            shift_ref[c, x] = moment[rows] / (mass + target)


def run_finish(like_dual, like_shift, *given):
    vmem = pl.BlockSpec(memory_space=pltpu.VMEM)
    return pl.pallas_call(
        finish_kernel,
        out_shape=tuple(jax.ShapeDtypeStruct(a.shape, jnp.float32) for a in (like_dual, like_shift)),
        in_specs=[vmem] * len(given),
        out_specs=(vmem, vmem),
        compiler_params=pltpu.CompilerParams(vmem_limit_bytes=4 * 2**20),
    )(*given)


def partner(kind, i, peers):
    if kind == "even":
        return i ^ 1
    if kind == "odd":
        return (i + 1 if i % 2 else i - 1) % peers
    if kind == "even2":
        return i ^ 2
    return (i + 2 if i % 4 >= 2 else i - 2) % peers


def swapped(array, axis, kind):
    peers = lax.axis_size(axis)
    return lax.ppermute(array, axis, [(i, partner(kind, i, peers)) for i in range(peers)])


def with_sides(array, axis):
    return jnp.concatenate([swapped(array, axis, "even"), array, swapped(array, axis, "odd")], 0)


def folded(array, axis):
    third = array.shape[0] // 3
    return (
        array[third : 2 * third]
        + swapped(array[:third], axis, "even")
        + swapped(array[2 * third :], axis, "odd")
    )


def folded_with_sides(blocks, axis):
    even, own, odd = blocks
    rows = own.shape[0]
    place = lax.axis_index(axis) % 4
    outer = (place == 0) | (place == 3)
    near_even = swapped(jnp.concatenate([own, even], 0), axis, "even")
    far_even = swapped(jnp.where(outer, even, odd), axis, "even2")
    near_odd = swapped(jnp.concatenate([own, odd], 0), axis, "odd")
    far_odd = swapped(jnp.where(outer, odd, even), axis, "odd2")
    return (
        near_even[:rows] + even + jnp.where(outer, far_even, far_odd),
        own + near_even[rows:] + near_odd[rows:],
        near_odd[:rows] + odd + jnp.where(outer, far_odd, far_even),
    )


def on_device(site_frac, dual_weight, target_mass, block_list, block_count):
    ways = [2 * (lax.axis_index(axis) % 2) - 1 for axis in ("gx", "gy")]
    ids = jnp.concatenate(
        [block_list.reshape(K_MAX), block_count.reshape(1), jnp.stack(ways).astype(jnp.int32)]
    )
    tile = lax.optimization_barrier(
        jnp.concatenate([site_frac, dual_weight[None], target_mass[None]], 0)
    )
    column, ids = lax.optimization_barrier((with_sides(tile, "gx"), ids))
    table = with_sides(column, "gy")

    partial = run_pass(ids, table)
    blocks = folded_with_sides([partial[i * ROWS : i * ROWS + 3 * INNER] for i in range(3)], "gx")
    rims = [
        jnp.concatenate([b[j * INNER : (j + 1) * INNER] for b in blocks], 0) for j in range(3)
    ]
    masses = jnp.concatenate(folded_with_sides(rims, "gy"), 0)

    spread, displacement = run_pass(ids, table, masses)
    summed = folded(spread, "gx")
    even = swapped(summed[: 4 * INNER], "gy", "even")
    odd = swapped(summed[8 * INNER :], "gy", "odd")
    new_dual, site_shift = run_finish(
        dual_weight, site_frac, tile, masses, summed, even, odd
    )
    return new_dual, site_shift, displacement


def solution(mesh):
    in_specs = (
        P(None, "gx", "gy", None),
        P("gx", "gy", None),
        P("gx", "gy", None),
        P("gx", "gy", None),
        P("gx", "gy"),
    )
    out_specs = (P("gx", "gy", None), P(None, "gx", "gy", None), P(None, "gx", "gy", None))
    return jax.shard_map(
        on_device, mesh=mesh, in_specs=in_specs, out_specs=out_specs, check_vma=False
    )
```
